256 devices in a mesh: rows: 64 (over z, y, core), grp: 4 (over x).
Axes of the slice: x: 4, y: 4, z: 8, core: 2. Of those that a mesh axis runs over, the one named last changes fastest.
Arguments:
- item_factors: bfloat16 [1048576, 128], P('rows'), may hold values from -120 to 120
- rated_owner: int32 [32768, 128], P(('rows', 'grp')), may hold values from 0 to 63, as said below
- rated_row: int32 [32768, 128], P(('rows', 'grp')), may hold values from 0 to 16383
- strength: float32 [32768, 128], P(('rows', 'grp')), may hold values from 0.1 to 3
Outputs:
- user_factors: float32 [32768, 128], P(('rows', 'grp'))
The draws below stay inside these ranges and needn't reach their ends.
Inputs may be any that keep to these rules, and one draw needn't show every extreme that they name: `rated_owner`: among the 16384 slots of one device's users, at most 512 name one block; one block is named exactly 512 times by every device.
All inputs are finite; a program needn't handle non-finite values.
Results may differ from the reference program's by a relative error of at most 0.009.
Values may be sent and summed in bfloat16 or wider, within the bound.
A program may use at most 64 MiB of HBM per device.

```python
import math
import jax
import jax.numpy as jnp
from jax import lax

R = 128
LMAX = 128
ITERS = 16
USER_BLOCK = 16
U_DEV = 128
ITEMS_ROW = 16384
USERS = 32768
ITEMS = 1048576
CAP = 512


def draw_rated_owner(key, part):
    key = jax.random.fold_in(key, 11)
    owners_count = ITEMS // ITEMS_ROW
    block_total = U_DEV * LMAX
    block_count = USERS // U_DEV
    hot_owner = jax.random.randint(jax.random.fold_in(key, 1), (), 0, owners_count).astype(jnp.int32)
    pool_index = jnp.arange((owners_count - 1) * CAP, dtype=jnp.int32) // CAP
    pool_owner = pool_index + (pool_index >= hot_owner).astype(jnp.int32)

    def one_block(block_key):
        key_pick, key_shuffle = jax.random.split(block_key, 2)
        chosen = jax.random.permutation(key_pick, pool_owner)[:block_total - CAP]
        owners = jnp.concatenate([jnp.full((CAP,), 1, jnp.int32) * hot_owner, chosen])
        owners = jax.random.permutation(key_shuffle, owners)
        return owners.reshape(U_DEV, LMAX)
    block_keys = jax.random.split(jax.random.fold_in(key, 2), block_count)
    return jax.vmap(one_block)(block_keys).reshape(USERS, LMAX).astype(jnp.int32)


def draw_rated_row(key, part):
    key = jax.random.fold_in(key, 17)
    return jax.random.randint(key, (USERS, LMAX), 0, ITEMS_ROW).astype(jnp.int32)


def draw_item_factors(key, part):
    key = jax.random.fold_in(key, 23)
    key_values, key_rows = jax.random.split(key, 2)
    position = jnp.arange(ITEMS, dtype=jnp.float32)[:, None] / ITEMS
    rising = jnp.exp(position * math.log(3.0))
    row_draw = jax.random.uniform(key_rows, (ITEMS, 1), jnp.float32, 0.0, 1.0)
    row_scale = 0.5 * jnp.exp(row_draw * math.log(10.0))
    values = jax.random.truncated_normal(key_values, -4.0, 4.0, (ITEMS, R), jnp.float32)
    return (values * row_scale * rising).astype(jnp.bfloat16)


def block_scale(stream_key, dims, cuts, low, largest):
    level, own = 1.0, jax.random.fold_in(stream_key, 6)
    for dim, parts in cuts:
        steps = jnp.exp(jax.random.uniform(jax.random.fold_in(own, dim), (parts,), jnp.float32, low / len(cuts), largest / len(cuts)))
        level = level * jnp.repeat(steps, dims[dim] // parts).reshape([-1 if axis == dim else 1 for axis in range(len(dims))])
    return level


def setup_inputs(seed: int = 0) -> dict:
    splits = jax.random.split(jax.random.key(seed), 5)
    return {
        "item_factors": draw_item_factors(jax.random.fold_in(splits[4], 71), 0),
        "rated_owner": draw_rated_owner(jax.random.fold_in(splits[4], 71), 0),
        "rated_row": draw_rated_row(jax.random.fold_in(splits[4], 71), 0),
        "strength": jnp.clip(jnp.exp(math.log(3.0) - 3.4011974 * jax.random.uniform(splits[3], (USERS, LMAX), jnp.float32) ** block_scale(splits[3], (USERS, LMAX), ((0, 256),), -0.2, 0.2)), 0.1, 3.0),
    }


ridge = 5.0
tiny = 1e-6


def conjugate(apply_system, target):
    def advance(index, carry):
        solution, residual, direction, norm_now = carry
        image = apply_system(direction)
        alpha = norm_now / (jnp.sum(direction * image, axis=1, keepdims=True) + tiny)
        solution = solution + alpha * direction
        residual = residual - alpha * image
        norm_next = jnp.sum(residual * residual, axis=1, keepdims=True)
        direction = residual + (norm_next / (norm_now + tiny)) * direction
        return (solution, residual, direction, norm_next)

    start = (jnp.zeros_like(target), target, target, jnp.sum(target * target, axis=1, keepdims=True))
    result = lax.fori_loop(0, ITERS, advance, start)
    return result[0]


def solve_block(gram_mean, slot_rows, weights):
    rows_wide = slot_rows.astype(jnp.float32)
    weighted = rows_wide * weights[:, :, None]
    system = LMAX * gram_mean[None] + jnp.einsum('usr,ust->urt', weighted, rows_wide, precision=lax.Precision.HIGHEST)
    system = system + ridge * jnp.eye(R, dtype=jnp.float32)[None]
    target = jnp.sum(rows_wide + weighted, axis=1)

    def apply_system(direction):
        return jnp.einsum('urt,ut->ur', system, direction, precision=lax.Precision.HIGHEST)

    return conjugate(apply_system, target)


def reference(item_factors, rated_owner, rated_row, strength):
    gram_mean = jnp.dot(item_factors.T, item_factors, preferred_element_type=jnp.float32) / ITEMS
    rated_items = (rated_owner * ITEMS_ROW + rated_row).astype(jnp.int32)
    block_count = USERS // USER_BLOCK
    grouped_items = rated_items.reshape(block_count, USER_BLOCK, LMAX)
    grouped_weights = strength.reshape(block_count, USER_BLOCK, LMAX)

    def one_block(pair):
        item_block, weight_block = pair
        slot_rows = jnp.take(item_factors, item_block, axis=0)
        return solve_block(gram_mean, slot_rows, weight_block)

    solved = lax.map(one_block, (grouped_items, grouped_weights))
    return solved.reshape(USERS, R)
```

```python
import functools
import jax
import jax.numpy as jnp
from jax import lax
from jax.experimental import pallas as pl
from jax.experimental.pallas import tpu as pltpu
from jax.sharding import PartitionSpec as P

f32, bf16, i32 = jnp.float32, jnp.bfloat16, jnp.int32
ITERS = 16
ridge = 5.0
tiny = 1e-6
MIB = 1024 * 1024


def prep_kernel(owners, cap, group, owner_ref, row_ref, place_ref, asked_ref, base, acc):
    users, slots = owner_ref.shape
    which = lax.broadcasted_iota(i32, (owners, slots), 0)
    before = lax.broadcasted_iota(i32, (slots, 2 * slots), 0)
    after = lax.broadcasted_iota(i32, (slots, 2 * slots), 1)
    earlier = jnp.where((before < after) | (after >= slots), 1.0, 0.0).astype(bf16)
    ranks = lax.broadcasted_iota(i32, (cap, slots), 0)
    base[...] = jnp.zeros_like(base)
    acc[...] = jnp.zeros_like(acc)

    def step(index, _):
        left, right = [], []
        for inner in range(group):
            user = index * group + inner
            own = owner_ref[pl.ds(user, 1), :]
            row = row_ref[pl.ds(user, 1), :]
            hot = jnp.where(which == own, 1.0, 0.0)
            counts = jnp.dot(hot.astype(bf16), earlier, preferred_element_type=f32)
            rank = jnp.sum(hot * (counts[:, :slots] + base[...]), axis=0, keepdims=True).astype(i32)
            base[...] += counts[:, slots:]
            place_ref[pl.ds(user, 1), :] = own * cap + rank
            high = (row // 128).astype(f32)
            low = (row % 128).astype(f32)
            left.append(jnp.concatenate([hot * high, hot * low], axis=0).astype(bf16))
            right.append(jnp.where(ranks == rank, 1.0, 0.0).astype(bf16))
        acc[...] += lax.dot_general(
            jnp.concatenate(left, axis=1),
            jnp.concatenate(right, axis=1),
            (((1,), (1,)), ((), ())),
            preferred_element_type=f32,
        )
        return 0

    lax.fori_loop(0, users // group, step, 0)
    total = acc[...]
    asked_ref[...] = (total[:owners] * 128.0 + total[owners:]).astype(i32)


def prepare(owner, row, owners, cap, group=16):
    users, slots = owner.shape
    return pl.pallas_call(
        functools.partial(prep_kernel, owners, cap, group),
        out_shape=(
            jax.ShapeDtypeStruct((users, slots), i32),
            jax.ShapeDtypeStruct((owners, cap), i32),
        ),
        in_specs=[pl.BlockSpec(memory_space=pltpu.VMEM)] * 2,
        out_specs=[pl.BlockSpec(memory_space=pltpu.VMEM)] * 2,
        scratch_shapes=[pltpu.VMEM((owners, slots), f32), pltpu.VMEM((2 * owners, cap), f32)],
        compiler_params=pltpu.CompilerParams(vmem_limit_bytes=32 * MIB),
    )(owner, row)


def split3(x):
    high = x.astype(bf16)
    rest = x - high.astype(f32)
    mid = rest.astype(bf16)
    low = (rest - mid.astype(f32)).astype(bf16)
    return high, mid, low


def conjugate(big, target, vec):
    rank, users = target.shape

    def apply_system():
        def part(index, acc):
            return acc + big[pl.ds(pl.multiple_of(index * rank, rank), rank), :] * vec[pl.ds(index, 1), :]
        return lax.fori_loop(0, rank, part, jnp.zeros((rank, users), f32), unroll=8)

    def advance(index, carry):
        solution, residual, norm_now = carry
        image = apply_system()
        direction = vec[...]
        alpha = norm_now / (jnp.sum(direction * image, axis=0, keepdims=True) + tiny)
        solution = solution + alpha * direction
        residual = residual - alpha * image
        norm_next = jnp.sum(residual * residual, axis=0, keepdims=True)
        vec[...] = residual + norm_next / (norm_now + tiny) * direction
        return solution, residual, norm_next

    vec[...] = target
    start = (jnp.zeros_like(target), target, jnp.sum(target * target, axis=0, keepdims=True))
    return lax.fori_loop(0, ITERS, advance, start)[0]


def solve_kernel(place, fetched, strength, gram, out, wide, rows, systems, big, targets, vec):
    users, slots = strength.shape
    rank = out.shape[1]
    fetch_total = wide.shape[0]
    step = 512

    def widen(index, _):
        at = pl.ds(pl.multiple_of(index * step, step), step)
        wide[at, :] = fetched[at, :].astype(f32)
        return 0

    lax.fori_loop(0, fetch_total // step, widen, 0)
    eye = jnp.where(
        lax.broadcasted_iota(i32, (rank, rank), 0) == lax.broadcasted_iota(i32, (rank, rank), 1), ridge, 0.0
    )
    shared = gram[...] + eye


    def some_users(index, _):
        helds = []
        for g in range(8):
            user = index * 8 + g
            for slot in range(slots):
                rows[pl.ds(g * slots + slot, 1), :] = wide[pl.ds(place[user * slots + slot], 1), :]
        for g in range(8):
            user = index * 8 + g
            held = rows[g * slots:(g + 1) * slots, :]
            short = held.astype(bf16)
            weights = strength[pl.ds(user, 1), :]
            turned = short.T.astype(f32)
            parts = split3(turned * weights)[:3]
            extra = split3(jnp.broadcast_to(1.0 + weights, (16, slots)))
            left = jnp.concatenate([*parts, *extra], axis=0)
            product = jnp.dot(left, short, preferred_element_type=f32)
            system = product[(3 - 1) * rank:3 * rank]
            for k in range(3 - 2, -1, -1):
                system = system + product[k * rank:(k + 1) * rank]
            systems[pl.ds(pl.multiple_of(user * rank, rank), rank), :] = system + shared
            tail = 3 * rank
            targets[pl.ds(user, 1), :] = (
                product[tail:tail + 1] + (product[tail + 16:tail + 17] + product[tail + 32:tail + 33])
            )
        return 0

    lax.fori_loop(0, users // 8, some_users, 0)

    def turn(index, _):
        block = systems[pl.ds(index, users, stride=rank), :]
        big[pl.ds(pl.multiple_of(index * rank, rank), rank), :] = block.T
        return 0

    lax.fori_loop(0, rank, turn, 0, unroll=8)
    out[...] = conjugate(big, targets[...].T, vec).T


def solve(place, fetched, strength, gram):
    users, slots = strength.shape
    total, rank = fetched.shape
    vmem = pl.BlockSpec(memory_space=pltpu.VMEM)
    return pl.pallas_call(
        solve_kernel,
        out_shape=jax.ShapeDtypeStruct((users, rank), f32),
        in_specs=[pl.BlockSpec(memory_space=pltpu.SMEM), vmem, vmem, vmem],
        out_specs=vmem,
        scratch_shapes=[
            pltpu.VMEM((total, rank), f32),
            pltpu.VMEM((8 * slots, rank), f32),
            pltpu.VMEM((users * rank, rank), f32),
            pltpu.VMEM((rank * rank, users), f32),
            pltpu.VMEM((users, rank), f32),
            pltpu.VMEM((rank, users), f32),
        ],
        compiler_params=pltpu.CompilerParams(vmem_limit_bytes=60 * MIB),
    )(place, fetched, strength, gram)


MESH = pl.DeviceIdType.MESH
LANES = 128


def exchange_kernel(cap, order, asked, table, out, got, idx, wide, block, send,
                    ask_send, ask_recv, idx_sem, row_send, row_recv, own_sem):
    me = lax.axis_index("rows")
    n = asked.shape[0]
    z, y, c = me // 8, (me // 2) % 4, me % 2

    def offset(step):
        if order == "zslow":
            return step // 8, (step // 2) % 4, step % 2
        if order == "pair":
            k = step % 8
            dz = (k + 1) // 2 * (1 - 2 * (k % 2))
            return (dz + 8) % 8, (step // 8) % 4, step // 32
        if order == "zfast":
            return step % 8, (step // 8) % 4, step // 32

    def ahead(step):
        dz, dy, dc = offset(step)
        return (((z + dz) % 8) * 4 + (y + dy) % 4) * 2 + (c + dc) % 2

    def behind(step):
        dz, dy, dc = offset(step)
        return (((z + 8 - dz) % 8) * 4 + (y + 4 - dy) % 4) * 2 + (c + 2 - dc) % 2

    barrier = pltpu.get_barrier_semaphore()

    def greet(step, _):
        pl.semaphore_signal(barrier, inc=1, device_id={"rows": ahead(step)}, device_id_type=MESH)
        return 0

    lax.fori_loop(1, n, greet, 0)
    pl.semaphore_wait(barrier, n - 1)

    def ask(step):
        return pltpu.make_async_remote_copy(
            src_ref=asked.at[ahead(step)], dst_ref=got.at[step], send_sem=ask_send.at[step],
            recv_sem=ask_recv.at[step], device_id={"rows": ahead(step)}, device_id_type=MESH)

    def ask_start(step, _):
        ask(step).start()
        return 0

    lax.fori_loop(1, n, ask_start, 0)

    part = 512

    def widen(index, _):
        at = pl.ds(pl.multiple_of(index * part, part), part)
        wide[at, :] = table[at, :].astype(f32)
        return 0

    lax.fori_loop(0, table.shape[0] // part, widen, 0)

    def fetch(slot, home):
        def rows(line, _):
            for inner in range(LANES):
                block[pl.ds(inner, 1), :] = wide[pl.ds(idx[slot, line, inner], 1), :]
            send[home, pl.ds(pl.multiple_of(line * LANES, LANES), LANES), :] = block[...].astype(bf16)
            return 0
        lax.fori_loop(0, cap // LANES, rows, 0)

    def answer(step):
        return pltpu.make_async_remote_copy(
            src_ref=send.at[step], dst_ref=out.at[me], send_sem=row_send.at[step],
            recv_sem=row_recv.at[step], device_id={"rows": behind(step)}, device_id_type=MESH)

    mine = pltpu.make_async_copy(asked.at[me], got.at[0], own_sem)
    mine.start()

    def asked_all(step, _):
        ask(step).wait_recv()
        return 0

    lax.fori_loop(1, n, asked_all, 0)
    mine.wait()
    numbers = pltpu.make_async_copy(got, idx, idx_sem)
    numbers.start()
    numbers.wait()

    def serve(step, _):
        fetch(step, step)
        answer(step).start()
        return 0

    lax.fori_loop(1, n, serve, 0)
    fetch(0, 0)
    own = pltpu.make_async_copy(send.at[0], out.at[me], own_sem)
    own.start()

    def finish(step, _):
        ask(step).wait_send()
        answer(step).wait_send()
        pltpu.make_async_remote_copy(
            src_ref=send.at[step], dst_ref=out.at[ahead(step)], send_sem=row_send.at[step],
            recv_sem=row_recv.at[step], device_id={"rows": ahead(step)}, device_id_type=MESH).wait_recv()
        return 0

    lax.fori_loop(1, n, finish, 0)
    own.wait()


def exchange(asked, table, order="pair", cid=0):
    owners, cap = asked.shape
    rows, rank = table.shape
    vmem = pl.BlockSpec(memory_space=pltpu.VMEM)
    dma = pltpu.SemaphoreType.DMA
    lines = cap // 128
    return pl.pallas_call(
        functools.partial(exchange_kernel, cap, order),
        out_shape=jax.ShapeDtypeStruct((owners, cap, rank), bf16),
        in_specs=[vmem, vmem],
        out_specs=pl.BlockSpec(memory_space=pl.ANY),
        scratch_shapes=[
            pltpu.VMEM((owners, lines, 128), i32),
            pltpu.SMEM((owners, lines, 128), i32),
            pltpu.VMEM((rows, rank), f32),
            pltpu.VMEM((LANES, rank), f32),
            pltpu.VMEM((owners, cap, rank), bf16),
            dma((owners,)), dma((owners,)), dma, dma((owners,)), dma((owners,)), dma,
        ],
        compiler_params=pltpu.CompilerParams(collective_id=cid, has_side_effects=True, vmem_limit_bytes=48 * MIB),
    )(asked.reshape(owners, lines, 128), table)


def per_device(item_factors, rated_owner, rated_row, strength):
    user_count, slot_count = rated_owner.shape
    shard_rows, rank = item_factors.shape
    owners = lax.axis_size("rows")
    cap = 2 * user_count * slot_count // owners
    place, asked = prepare(rated_owner, rated_row, owners, cap)
    copies = lax.axis_size("grp")
    share = shard_rows // copies
    piece = lax.dynamic_slice_in_dim(item_factors, lax.axis_index("grp") * share, share, 0)
    partial_gram = jnp.einsum("ir,it->rt", piece, piece, preferred_element_type=jnp.float32)
    gram_total = lax.psum(partial_gram, ("rows", "grp"))
    gram_weighted = slot_count * (gram_total / (shard_rows * owners))
    fetched = exchange(asked, item_factors)
    return solve(place.reshape(-1), fetched.reshape(owners * cap, rank), strength, gram_weighted)


def solution(mesh):
    placed = (P("rows", None), P(("rows", "grp"), None), P(("rows", "grp"), None), P(("rows", "grp"), None))
    return jax.shard_map(
        per_device, mesh=mesh, in_specs=placed, out_specs=P(("rows", "grp"), None), check_vma=False
    )
```

```python
import functools
import jax
import jax.numpy as jnp
from jax import lax
from jax.experimental import pallas as pl
from jax.experimental.pallas import tpu as pltpu
from jax.sharding import PartitionSpec as P

f32, bf16, i32 = jnp.float32, jnp.bfloat16, jnp.int32
ITERS = 16
ridge = 5.0
tiny = 1e-6
MIB = 1024 * 1024


CAP_PART = 5
NEAR = 24


def prep_kernel(owners, cap, spare, group, owner_ref, row_ref, place_ref, asked_ref, hot_ref, wrong_ref, base, acc, ranks):
    users, slots = owner_ref.shape
    full = cap + spare
    which = lax.broadcasted_iota(i32, (owners, slots), 0)
    before = lax.broadcasted_iota(i32, (slots, 2 * slots), 0)
    after = lax.broadcasted_iota(i32, (slots, 2 * slots), 1)
    earlier = jnp.where((before < after) | (after >= slots), 1.0, 0.0).astype(bf16)
    base[...] = jnp.zeros_like(base)
    acc[...] = jnp.zeros_like(acc)
    columns = lax.broadcasted_iota(i32, (full, slots), 0)

    def step(index, _):
        left, right = [], []
        for inner in range(group):
            user = index * group + inner
            own = owner_ref[pl.ds(user, 1), :]
            row = row_ref[pl.ds(user, 1), :]
            named = jnp.where(which == own, 1.0, 0.0)
            counts = jnp.dot(named.astype(bf16), earlier, preferred_element_type=f32)
            rank = jnp.sum(named * (counts[:, :slots] + base[...]), axis=0, keepdims=True).astype(i32)
            base[...] += counts[:, slots:]
            ranks[pl.ds(user, 1), :] = rank
            high = (row // 128).astype(f32)
            low = (row % 128).astype(f32)
            left.append(jnp.concatenate([named * high, named * low], axis=0).astype(bf16))
            right.append(jnp.where(columns == rank, 1.0, 0.0).astype(bf16))
        acc[...] += lax.dot_general(
            jnp.concatenate(left, axis=1),
            jnp.concatenate(right, axis=1),
            (((1,), (1,)), ((), ())),
            preferred_element_type=f32,
        )
        return 0

    lax.fori_loop(0, users // group, step, 0)
    counts = base[...].astype(i32)
    hot = jnp.min(jnp.where(counts == jnp.max(counts), which, owners))
    hot_ref[0, 0] = hot
    own, rank = owner_ref[...], ranks[...]
    past = rank >= cap
    place_ref[...] = jnp.where(past & (own == hot), owners * cap - cap + rank, own * cap + jnp.minimum(rank, cap - 1))
    bad = jnp.sum(jnp.where(past & (own != hot), 1.0, 0.0))
    wrong_ref[...] = jnp.zeros_like(wrong_ref) + bad
    total = acc[...]
    asked = (total[:owners] * 128.0 + total[owners:]).astype(i32)
    for line in range(full // 128):
        asked_ref[:, line, :] = asked[:, line * 128:(line + 1) * 128]


def prepare(owner, row, owners, cap, spare, group=16):
    users, slots = owner.shape
    full = cap + spare
    vmem = pl.BlockSpec(memory_space=pltpu.VMEM)
    return pl.pallas_call(
        functools.partial(prep_kernel, owners, cap, spare, group),
        out_shape=(
            jax.ShapeDtypeStruct((users, slots), i32),
            jax.ShapeDtypeStruct((owners, full // 128, 128), i32),
            jax.ShapeDtypeStruct((1, 1), i32),
            jax.ShapeDtypeStruct((8, slots), f32),
        ),
        in_specs=[vmem, vmem],
        out_specs=(vmem, vmem, pl.BlockSpec(memory_space=pltpu.SMEM), vmem),
        scratch_shapes=[
            pltpu.VMEM((owners, slots), f32),
            pltpu.VMEM((2 * owners, full), f32),
            pltpu.VMEM((users, slots), i32),
        ],
        compiler_params=pltpu.CompilerParams(vmem_limit_bytes=32 * MIB),
    )(owner, row)


def split3(x):
    high = x.astype(bf16)
    rest = x - high.astype(f32)
    mid = rest.astype(bf16)
    low = (rest - mid.astype(f32)).astype(bf16)
    return high, mid, low


def conjugate(big, target, vec):
    rank, users = target.shape

    def apply_system():
        def part(index, acc):
            return acc + big[pl.ds(pl.multiple_of(index * rank, rank), rank), :] * vec[pl.ds(index, 1), :]
        return lax.fori_loop(0, rank, part, jnp.zeros((rank, users), f32), unroll=8)

    def advance(index, carry):
        solution, residual, norm_now = carry
        image = apply_system()
        direction = vec[...]
        alpha = norm_now / (jnp.sum(direction * image, axis=0, keepdims=True) + tiny)
        solution = solution + alpha * direction
        residual = residual - alpha * image
        norm_next = jnp.sum(residual * residual, axis=0, keepdims=True)
        vec[...] = residual + norm_next / (norm_now + tiny) * direction
        return solution, residual, norm_next

    vec[...] = target
    start = (jnp.zeros_like(target), target, jnp.sum(target * target, axis=0, keepdims=True))
    return lax.fori_loop(0, ITERS, advance, start)[0]


def solve_kernel(gram_scale, place, fetched, strength, gram, out, wide, rows, systems, big, targets, vec):
    users, slots = strength.shape
    rank = out.shape[1]
    fetch_total = wide.shape[0]
    step = max(size for size in range(16, 1200, 16) if fetch_total % size == 0)

    def widen(index, _):
        at = pl.ds(pl.multiple_of(index * step, step), step)
        wide[at, :] = fetched[at, :].astype(f32)
        return 0

    lax.fori_loop(0, fetch_total // step, widen, 0)
    eye = jnp.where(
        lax.broadcasted_iota(i32, (rank, rank), 0) == lax.broadcasted_iota(i32, (rank, rank), 1), ridge, 0.0
    )
    shared = gram[:rank, :] * gram_scale + eye


    def some_users(index, _):
        helds = []
        for g in range(8):
            user = index * 8 + g
            for slot in range(slots):
                rows[pl.ds(g * slots + slot, 1), :] = wide[pl.ds(place[user * slots + slot], 1), :]
        for g in range(8):
            user = index * 8 + g
            held = rows[g * slots:(g + 1) * slots, :]
            short = held.astype(bf16)
            weights = strength[pl.ds(user, 1), :]
            turned = short.T.astype(f32)
            parts = split3(turned * weights)[:3]
            extra = split3(jnp.broadcast_to(1.0 + weights, (16, slots)))
            left = jnp.concatenate([*parts, *extra], axis=0)
            product = jnp.dot(left, short, preferred_element_type=f32)
            system = product[(3 - 1) * rank:3 * rank]
            for k in range(3 - 2, -1, -1):
                system = system + product[k * rank:(k + 1) * rank]
            systems[pl.ds(pl.multiple_of(user * rank, rank), rank), :] = system + shared
            tail = 3 * rank
            targets[pl.ds(user, 1), :] = (
                product[tail:tail + 1] + (product[tail + 16:tail + 17] + product[tail + 32:tail + 33])
            )
        return 0

    lax.fori_loop(0, users // 8, some_users, 0)

    def turn(index, _):
        block = systems[pl.ds(index, users, stride=rank), :]
        big[pl.ds(pl.multiple_of(index * rank, rank), rank), :] = block.T
        return 0

    lax.fori_loop(0, rank, turn, 0, unroll=8)
    out[...] = conjugate(big, targets[...].T, vec).T


def solve(place, fetched, strength, gram, gram_scale):
    users, slots = strength.shape
    total, rank = fetched.shape
    vmem = pl.BlockSpec(memory_space=pltpu.VMEM)
    return pl.pallas_call(
        functools.partial(solve_kernel, gram_scale),
        out_shape=jax.ShapeDtypeStruct((users, rank), f32),
        in_specs=[pl.BlockSpec(memory_space=pltpu.SMEM), vmem, vmem, vmem],
        out_specs=vmem,
        scratch_shapes=[
            pltpu.VMEM((total, rank), f32),
            pltpu.VMEM((8 * slots, rank), f32),
            pltpu.VMEM((users * rank, rank), f32),
            pltpu.VMEM((rank * rank, users), f32),
            pltpu.VMEM((users, rank), f32),
            pltpu.VMEM((rank, users), f32),
        ],
        compiler_params=pltpu.CompilerParams(vmem_limit_bytes=60 * MIB),
    )(place, fetched, strength, gram)


MESH = pl.DeviceIdType.MESH
LANES = 128
PIECE = 8


def exchange_kernel(cap, spare, near, asked, hot, wrong, table, out, sums, got, idx, wide, block, send,
                    gram_send, gram_got, gram_far, core_buf, core_send, y_send, y_buf, z_send, z_buf, last,
                    ask_send, ask_recv, row_send, row_recv, gram_sems, sum_sems, far_sems, hop_sems, copy_sems):
    me, copy_id = lax.axis_index("rows"), lax.axis_index("grp")
    copies = lax.axis_size("grp")
    n = asked.shape[0]
    z, y, c = me // 8, (me // 2) % 4, me % 2
    full = cap + spare

    def offset(step):
        k = step % 8
        dz = (k + 1) // 2 * (1 - 2 * (k % 2))
        return (dz + 8) % 8, (step // 8) % 4, step // 32

    def index_of(pz, py, pc):
        return (pz * 4 + py) * 2 + pc

    def ahead(step):
        dz, dy, dc = offset(step)
        return index_of((z + dz) % 8, (y + dy) % 4, (c + dc) % 2)

    def behind(step):
        dz, dy, dc = offset(step)
        return index_of((z + 8 - dz) % 8, (y + 4 - dy) % 4, (c + 2 - dc) % 2)

    def loop(low, high, body):
        def run(step, _):
            body(step)
            return 0
        lax.fori_loop(low, high, run, 0)

    def remote(src, dst, first, second, **device_id):
        return pltpu.make_async_remote_copy(
            src_ref=src, dst_ref=dst, send_sem=first, recv_sem=second,
            device_id=device_id, device_id_type=MESH)

    barrier = pltpu.get_barrier_semaphore()
    loop(1, n, lambda step: pl.semaphore_signal(
        barrier, inc=1, device_id={"rows": ahead(step)}, device_id_type=MESH))
    loop(1, copies, lambda step: pl.semaphore_signal(
        barrier, inc=1, device_id={"grp": (copy_id + step) % copies}, device_id_type=MESH))
    pl.semaphore_wait(barrier, n + copies - 2)

    def ask(step):
        return remote(asked.at[ahead(step)], got.at[step], ask_send.at[step], ask_recv.at[step], rows=ahead(step))

    loop(1, n, lambda step: ask(step).start())
    mine = pltpu.make_async_copy(asked.at[me], got.at[0], copy_sems.at[0])
    mine.start()

    share = table.shape[0] // copies
    part = 512

    def gram_part(index, acc):
        rows = table[pl.ds(pl.multiple_of(copy_id * share + index * part, part), part), :]
        return acc + lax.dot_general(rows, rows, (((0,), (0,)), ((), ())), preferred_element_type=f32)

    rank = table.shape[1]
    gram_send[:rank, :] = lax.fori_loop(0, share // part, gram_part, jnp.zeros((rank, rank), f32))
    gram_send[rank:, :] = wrong[...]
    pieces = gram_send.shape[0] // PIECE

    def piece(ref, index):
        return ref.at[pl.ds(pl.multiple_of(index * PIECE, PIECE), PIECE)]

    def gram_out(index):
        return remote(piece(gram_send, index), gram_got.at[me], gram_sems.at[0, index], gram_sems.at[1, me], rows=3 * index)

    def gram_start(index):
        @pl.when(3 * index != me)
        def _():
            gram_out(index).start()

    loop(0, pieces, gram_start)

    def widen(index):
        at = pl.ds(pl.multiple_of(index * part, part), part)
        wide[at, :] = table[at, :].astype(f32)

    loop(0, table.shape[0] // part, widen)
    loop(1, n, lambda step: ask(step).wait_recv())
    mine.wait()
    numbers = pltpu.make_async_copy(got, idx, copy_sems.at[0])
    numbers.start()
    numbers.wait()

    def fetch(step, line, first, count, dst, at):
        for inner in range(count):
            block[pl.ds(inner, 1), :] = wide[pl.ds(idx[step, line, first + inner], 1), :]
        dst[pl.ds(at, count), :] = block[:count, :].astype(bf16)

    lines, rest = cap // LANES, cap % LANES

    def serve_rows(step):
        loop(0, lines, lambda line: fetch(
            step, line, 0, LANES, send.at[step], pl.multiple_of(line * LANES, LANES)))
        if rest:
            fetch(step, lines, 0, rest, send.at[step], lines * LANES)

    def answer(step):
        return remote(send.at[step], out.at[pl.ds(pl.multiple_of(me * cap, 16), cap)],
                      row_send.at[step], row_recv.at[step], rows=behind(step))

    def answered(step):
        return remote(send.at[step], out.at[pl.ds(pl.multiple_of(ahead(step) * cap, 16), cap)],
                      row_send.at[step], row_recv.at[step], rows=ahead(step))

    def serve(step):
        serve_rows(step)
        answer(step).start()

    def spare_rows(step, dst):
        at = 0
        line, first = lines, rest
        while at < spare:
            count = min(LANES - first, spare - at)
            fetch(step, line, first, count, dst, at)
            at, line, first = at + count, line + 1, 0

    def column(step):
        dz, dy, dc = offset(step)
        return ((y + 4 - dy) % 4) * 8 + (z + 8 - dz) % 8

    half = n // 2
    loop(1, near, serve)
    loop(half, n, lambda step: spare_rows(step, core_send.at[column(step)]))
    core_hop = remote(core_send, core_buf.at[c], hop_sems.at[0], hop_sems.at[1], rows=index_of(z, y, 1 - c))
    core_hop.start()
    loop(0, half, lambda step: spare_rows(step, core_buf.at[c, column(step)]))
    loop(near, n, serve)
    serve_rows(0)
    own = pltpu.make_async_copy(send.at[0], out.at[pl.ds(pl.multiple_of(me * cap, 16), cap)], copy_sems.at[0])
    own.start()

    named = hot[0, 0]
    hot_z, hot_y, hot_c = named // 8, (named // 2) % 4, named % 2

    core_hop.wait()

    def keep_core(index):
        y_send[index] = core_buf[hot_c, index]

    loop(0, half, keep_core)

    def y_hop(dy):
        py = (y + dy) % 4
        return remote(y_send.at[pl.ds(py * 8, 8)], y_buf.at[pl.ds(y * 8, 8)], hop_sems.at[2 * dy], hop_sems.at[2 * dy + 1],
                      rows=index_of(z, py, c))

    for dy in (1, 2, 3):
        y_hop(dy).start()

    owner = (me % 3 == 0) & (me < 3 * pieces)

    @pl.when(owner)
    def _():
        gram_got[me] = gram_send[pl.ds(pl.multiple_of(me // 3 * PIECE, PIECE), PIECE), :]

        def gram_in(index):
            @pl.when(index != me)
            def _():
                remote(piece(gram_send, 0), gram_got.at[index], gram_sems.at[0, 0], gram_sems.at[1, index],
                       rows=index).wait_recv()

        loop(0, n, gram_in)
        gram_far[copy_id] = lax.fori_loop(
            0, n, lambda index, acc: acc + gram_got[index], jnp.zeros((PIECE, rank), f32))

        def far(step):
            return remote(gram_far.at[copy_id], gram_far.at[copy_id], far_sems.at[0, step], far_sems.at[1, step],
                          grp=(copy_id + step) % copies)

        for step in range(1, 4):
            far(step).start()
        for step in range(1, 4):
            far(step).wait()
        total = gram_far[0]
        for index in range(1, 4):
            total = total + gram_far[index]
        sums[pl.ds(pl.multiple_of(me // 3 * PIECE, PIECE), PIECE), :] = total

    def spread(step):
        at = piece(sums, me // 3)
        return remote(at, at, sum_sems.at[0, step], sum_sems.at[1, me // 3], rows=ahead(step))

    @pl.when(owner)
    def _():
        loop(1, n, lambda step: spread(step).start())

    for dy in (1, 2, 3):
        y_hop(dy).wait()

    def keep_y(index):
        y_buf[y * 8 + index] = y_send[y * 8 + index]

    loop(0, 8, keep_y)

    def keep_z(index):
        z_send[index] = y_buf[hot_y * 8 + index]

    loop(0, 8, keep_z)

    def z_hop(dz):
        pz = (z + dz) % 8
        return remote(z_send.at[pz], z_buf.at[z], hop_sems.at[8 + 2 * dz], hop_sems.at[9 + 2 * dz],
                      rows=index_of(pz, y, c))

    loop(1, 8, lambda dz: z_hop(dz).start())
    z_buf[z] = z_send[z]

    def finish(step):
        ask(step).wait_send()
        answer(step).wait_send()
        answered(step).wait_recv()

    loop(1, n, finish)
    loop(1, 8, lambda dz: z_hop(dz).wait())
    own.wait()
    last[...] = z_buf[hot_z]
    tail = pltpu.make_async_copy(last, out.at[pl.ds(n * cap, spare)], copy_sems.at[0])
    tail.start()
    tail.wait()

    def gram_sent(index):
        @pl.when(3 * index != me)
        def _():
            gram_out(index).wait_send()
            at = piece(sums, index)
            remote(at, at, sum_sems.at[0, 0], sum_sems.at[1, index], rows=3 * index).wait_recv()

    loop(0, pieces, gram_sent)

    @pl.when(owner)
    def _():
        loop(1, n, lambda step: spread(step).wait_send())


def exchange(asked, hot, wrong, table, cap, spare, copies, near):
    owners, lines, _ = asked.shape
    rows, rank = table.shape
    vmem = pl.BlockSpec(memory_space=pltpu.VMEM)
    dma = pltpu.SemaphoreType.DMA
    half = owners // 2
    pieces = rank // PIECE + 1
    return pl.pallas_call(
        functools.partial(exchange_kernel, cap, spare, near),
        out_shape=(
            jax.ShapeDtypeStruct((owners * cap + spare, rank), bf16),
            jax.ShapeDtypeStruct((pieces * PIECE, rank), f32),
        ),
        in_specs=[vmem, pl.BlockSpec(memory_space=pltpu.SMEM), vmem, vmem],
        out_specs=(pl.BlockSpec(memory_space=pl.ANY), vmem),
        scratch_shapes=[
            pltpu.VMEM((owners, lines, LANES), i32),
            pltpu.SMEM((owners, lines, LANES), i32),
            pltpu.VMEM((rows, rank), f32),
            pltpu.VMEM((LANES, rank), f32),
            pltpu.VMEM((owners, cap, rank), bf16),
            pltpu.VMEM((pieces * PIECE, rank), f32),
            pltpu.VMEM((owners, PIECE, rank), f32),
            pltpu.VMEM((copies, PIECE, rank), f32),
            pltpu.VMEM((2, half, spare, rank), bf16),
            pltpu.VMEM((half, spare, rank), bf16),
            pltpu.VMEM((half, spare, rank), bf16),
            pltpu.VMEM((half, spare, rank), bf16),
            pltpu.VMEM((8, spare, rank), bf16),
            pltpu.VMEM((8, spare, rank), bf16),
            pltpu.VMEM((spare, rank), bf16),
            dma((owners,)), dma((owners,)), dma((owners,)), dma((owners,)),
            dma((2, owners)), dma((2, owners)), dma((2, 4)), dma((24,)), dma((1,)),
        ],
        compiler_params=pltpu.CompilerParams(collective_id=0, has_side_effects=True, vmem_limit_bytes=48 * MIB),
    )(asked, hot, wrong, table)


def fetch_any(item_factors, rated_owner, rated_row):
    owners = lax.axis_size("rows")
    slot_owner = rated_owner.reshape(-1)
    local_row = rated_row.reshape(-1)
    slot_total = slot_owner.shape[0]
    rank = item_factors.shape[1]
    capacity = 2 * slot_total // owners
    slot_order = jnp.argsort(slot_owner, stable=True)
    sorted_owner = slot_owner[slot_order]
    owner_starts = jnp.searchsorted(sorted_owner, jnp.arange(owners, dtype=jnp.int32))
    sorted_rank = jnp.arange(slot_total, dtype=jnp.int32) - owner_starts[sorted_owner]
    sorted_place = sorted_owner * capacity + sorted_rank
    bucket_slot = jnp.zeros((slot_total,), jnp.int32).at[slot_order].set(sorted_place)
    asked_rows = jnp.zeros((owners * capacity,), jnp.int32).at[bucket_slot].set(local_row)
    asked_rows = asked_rows.reshape(owners, capacity)
    found = jnp.take(
        item_factors,
        lax.all_to_all(asked_rows, "rows", split_axis=0, concat_axis=0, tiled=True),
        axis=0,
    )
    fetched = lax.all_to_all(found, "rows", split_axis=0, concat_axis=0, tiled=True)
    return jnp.take(fetched.reshape(owners * capacity, rank), bucket_slot, axis=0)


def per_device(item_factors, rated_owner, rated_row, strength):
    user_count, slot_count = rated_owner.shape
    shard_rows, rank = item_factors.shape
    owners = lax.axis_size("rows")
    most = 2 * user_count * slot_count // owners
    cap = most * CAP_PART // 8
    place, asked, hot, wrong = prepare(rated_owner, rated_row, owners, cap, most - cap)
    fetched, sums = exchange(asked, hot, wrong, item_factors, cap, most - cap, lax.axis_size("grp"), NEAR)
    scale = slot_count / (shard_rows * owners)

    def usual(_):
        return solve(place.reshape(-1), fetched, strength, sums, scale)

    def any_counts(_):
        rows = fetch_any(item_factors, rated_owner, rated_row)
        return solve(jnp.arange(user_count * slot_count, dtype=jnp.int32), rows, strength, sums, scale)

    return lax.cond(sums[rank, 0] == 0.0, usual, any_counts, 0)


def solution(mesh):
    placed = (P("rows", None), P(("rows", "grp"), None), P(("rows", "grp"), None), P(("rows", "grp"), None))
    return jax.shard_map(
        per_device, mesh=mesh, in_specs=placed, out_specs=P(("rows", "grp"), None), check_vma=False
    )
```

```python
import functools
import jax
import jax.numpy as jnp
from jax import lax
from jax.experimental import pallas as pl
from jax.experimental.pallas import tpu as pltpu
from jax.sharding import PartitionSpec as P

f32, bf16, i32 = jnp.float32, jnp.bfloat16, jnp.int32
ITERS = 16
ridge = 5.0
tiny = 1e-6
MIB = 1024 * 1024


NEAR = (12, 24, 40, 64, 48)
GROUP = 8


def prep_kernel(owners, early, late, spare, early_users, group, owner_ref, row_ref, place_ref, asked_ref, hot_ref, wrong_ref, base, acc, ranks):
    users, slots = owner_ref.shape
    cap = early + late
    full = cap + spare
    which = lax.broadcasted_iota(i32, (owners, slots), 0)
    before = lax.broadcasted_iota(i32, (slots, 2 * slots), 0)
    after = lax.broadcasted_iota(i32, (slots, 2 * slots), 1)
    earlier = jnp.where((before < after) | (after >= slots), 1.0, 0.0).astype(bf16)
    base[...] = jnp.zeros_like(base)
    acc[...] = jnp.zeros_like(acc)
    columns = lax.broadcasted_iota(i32, (full, slots), 0)

    def step(index, _):
        left, right = [], []
        for inner in range(group):
            user = index * group + inner
            own = owner_ref[pl.ds(user, 1), :]
            row = row_ref[pl.ds(user, 1), :]
            named = jnp.where(which == own, 1.0, 0.0)
            counts = jnp.dot(named.astype(bf16), earlier, preferred_element_type=f32)
            rank = jnp.sum(named * (counts[:, :slots] + base[...]), axis=0, keepdims=True).astype(i32)
            base[...] += counts[:, slots:]
            ranks[pl.ds(user, 1), :] = rank
            high = (row // 128).astype(f32)
            low = (row % 128).astype(f32)
            left.append(jnp.concatenate([named * high, named * low], axis=0).astype(bf16))
            right.append(jnp.where(columns == rank, 1.0, 0.0).astype(bf16))
        acc[...] += lax.dot_general(
            jnp.concatenate(left, axis=1),
            jnp.concatenate(right, axis=1),
            (((1,), (1,)), ((), ())),
            preferred_element_type=f32,
        )
        return 0

    lax.fori_loop(0, users // group, step, 0)
    counts = base[...].astype(i32)
    hot = jnp.min(jnp.where(counts == jnp.max(counts), which, owners))
    hot_ref[0, 0] = hot
    own, rank = owner_ref[...], ranks[...]
    favoured = own == hot
    user = lax.broadcasted_iota(i32, rank.shape, 0)
    first = user < early_users
    spot = jnp.where(
        favoured & (rank >= early),
        jnp.where(rank < early + spare, rank + late, rank - spare),
        jnp.where(favoured, rank, jnp.minimum(rank, cap - 1)),
    )
    late_base = owners * early
    place_ref[...] = jnp.where(
        spot < early,
        own * early + spot,
        jnp.where(spot < cap, late_base + own * late + spot - early, late_base + owners * late + spot - cap),
    )
    limit = jnp.where(
        favoured, jnp.where(first, early + spare, full), jnp.where(first, early, cap))
    bad = jnp.sum(jnp.where(rank >= limit, 1.0, 0.0))
    wrong_ref[...] = jnp.zeros_like(wrong_ref) + bad
    total = acc[...]
    asked = (total[:owners] * 128.0 + total[owners:]).astype(i32)
    moved = jnp.concatenate([asked[:, :early], asked[:, early + spare:], asked[:, early:early + spare]], axis=1)
    asked = jnp.where(lax.broadcasted_iota(i32, asked.shape, 0) == hot, moved, asked)
    for line in range(full // 128):
        asked_ref[:, line, :] = asked[:, line * 128:(line + 1) * 128]


def prepare(owner, row, owners, early, late, spare, early_users, group=16):
    users, slots = owner.shape
    full = early + late + spare
    vmem = pl.BlockSpec(memory_space=pltpu.VMEM)
    return pl.pallas_call(
        functools.partial(prep_kernel, owners, early, late, spare, early_users, group),
        out_shape=(
            jax.ShapeDtypeStruct((users, slots), i32),
            jax.ShapeDtypeStruct((owners, full // 128, 128), i32),
            jax.ShapeDtypeStruct((1, 1), i32),
            jax.ShapeDtypeStruct((8, slots), f32),
        ),
        in_specs=[vmem, vmem],
        out_specs=(vmem, vmem, pl.BlockSpec(memory_space=pltpu.SMEM), vmem),
        scratch_shapes=[
            pltpu.VMEM((owners, slots), f32),
            pltpu.VMEM((2 * owners, full), f32),
            pltpu.VMEM((users, slots), i32),
        ],
        compiler_params=pltpu.CompilerParams(vmem_limit_bytes=32 * MIB),
    )(owner, row)


def split3(x):
    high = x.astype(bf16)
    rest = x - high.astype(f32)
    mid = rest.astype(bf16)
    low = (rest - mid.astype(f32)).astype(bf16)
    return high, mid, low


def conjugate(big, target, vec):
    rank, users = target.shape

    def apply_system():
        def part(index, acc):
            return acc + big[pl.ds(pl.multiple_of(index * rank, rank), rank), :] * vec[pl.ds(index, 1), :]
        return lax.fori_loop(0, rank, part, jnp.zeros((rank, users), f32), unroll=8)

    def advance(index, carry):
        solution, residual, norm_now = carry
        image = apply_system()
        direction = vec[...]
        alpha = norm_now / (jnp.sum(direction * image, axis=0, keepdims=True) + tiny)
        solution = solution + alpha * direction
        residual = residual - alpha * image
        norm_next = jnp.sum(residual * residual, axis=0, keepdims=True)
        vec[...] = residual + norm_next / (norm_now + tiny) * direction
        return solution, residual, norm_next

    vec[...] = target
    start = (jnp.zeros_like(target), target, jnp.sum(target * target, axis=0, keepdims=True))
    return lax.fori_loop(0, ITERS, advance, start)[0]


def widen_rows(source, target, base):
    total = source.shape[0]
    size = max(part for part in range(16, 1040, 16) if total % part == 0)

    def part(index, _):
        at = pl.multiple_of(index * size, size)
        target[pl.ds(base + at, size), :] = source[pl.ds(at, size), :].astype(f32)
        return 0

    lax.fori_loop(0, total // size, part, 0)


def gram_shared(sums, scale):
    rank = sums.shape[1]
    same = lax.broadcasted_iota(i32, (rank, rank), 0) == lax.broadcasted_iota(i32, (rank, rank), 1)
    return sums[:rank, :] * scale + jnp.where(same, ridge, 0.0)


def build_systems(first, last, place, wide, strength, rows, systems, targets):
    slots, rank = strength.shape[1], systems.shape[1]

    def some_users(index, _):
        for g in range(GROUP):
            user = index * GROUP + g
            for slot in range(slots):
                rows[pl.ds(g * slots + slot, 1), :] = wide[pl.ds(place[user * slots + slot], 1), :]
        for g in range(GROUP):
            user = index * GROUP + g
            short = rows[g * slots:(g + 1) * slots, :].astype(bf16)
            weights = strength[pl.ds(user, 1), :]
            extra = split3(jnp.broadcast_to(1.0 + weights, (16, slots)))
            left = jnp.concatenate([*split3(short.T.astype(f32) * weights), *extra], axis=0)
            product = jnp.dot(left, short, preferred_element_type=f32)
            system = product[2 * rank:3 * rank] + product[rank:2 * rank] + product[:rank]
            systems[pl.ds(pl.multiple_of(user * rank, rank), rank), :] = system
            tail = 3 * rank
            targets[pl.ds(user, 1), :] = (
                product[tail:tail + 1] + (product[tail + 16:tail + 17] + product[tail + 32:tail + 33])
            )
        return 0

    lax.fori_loop(first // GROUP, last // GROUP, some_users, 0)


def solve_systems(shared, systems, big, targets, vec):
    users, rank = targets.shape

    def turn(index, _):
        block = systems[pl.ds(index, users, stride=rank), :] + shared[pl.ds(index, 1), :]
        big[pl.ds(pl.multiple_of(index * rank, rank), rank), :] = block.T
        return 0

    lax.fori_loop(0, rank, turn, 0, unroll=8)
    return conjugate(big, targets[...].T, vec).T


def solve_kernel(scale, place, fetched, strength, sums, out, wide, shared, rows, systems, big, targets, vec):
    widen_rows(fetched, wide, 0)
    build_systems(0, strength.shape[0], place, wide, strength, rows, systems, targets)
    shared[...] = gram_shared(sums, scale)
    out[...] = solve_systems(shared, systems, big, targets, vec)


def solve(place, fetched, strength, gram, gram_scale):
    users, slots = strength.shape
    total, rank = fetched.shape
    vmem = pl.BlockSpec(memory_space=pltpu.VMEM)
    return pl.pallas_call(
        functools.partial(solve_kernel, gram_scale),
        out_shape=jax.ShapeDtypeStruct((users, rank), f32),
        in_specs=[pl.BlockSpec(memory_space=pltpu.SMEM), vmem, vmem, vmem],
        out_specs=vmem,
        scratch_shapes=[
            pltpu.VMEM((total, rank), f32),
            pltpu.VMEM((rank, rank), f32),
            pltpu.VMEM((8 * slots, rank), f32),
            pltpu.VMEM((users * rank, rank), f32),
            pltpu.VMEM((rank * rank, users), f32),
            pltpu.VMEM((users, rank), f32),
            pltpu.VMEM((rank, users), f32),
        ],
        compiler_params=pltpu.CompilerParams(vmem_limit_bytes=60 * MIB),
    )(place, fetched, strength, gram)


MESH = pl.DeviceIdType.MESH
LANES = 128
PIECE = 8


def exchange_kernel(early, late, spare, early_users, near, scale, asked, hot, wrong, place_in, strength, table_in,
                    out, sums, got, idx, place, table, wide, block, send_early, send_late, got_early, got_late,
                    gram_send, gram_got, gram_far, core_buf, core_send, y_send, y_buf, z_send, z_buf,
                    fetched, rows, systems, targets, vec,
                    ask_send, ask_recv, early_send, early_recv, late_send, late_recv, gram_sems, sum_sems, far_sems,
                    hop_sems, copy_sems):
    me, copy_id = lax.axis_index("rows"), lax.axis_index("grp")
    copies = lax.axis_size("grp")
    n = asked.shape[0]
    z, y, c = me // 8, (me // 2) % 4, me % 2
    cap = early + late
    table_copy = pltpu.make_async_copy(table_in, table, copy_sems.at[1])
    table_copy.start()
    place_copy = pltpu.make_async_copy(place_in, place, copy_sems.at[2])
    place_copy.start()

    def offset(step):
        k = step % 8
        dz = (k + 1) // 2 * (1 - 2 * (k % 2))
        return (dz + 8) % 8, (step // 8) % 4, step // 32

    def index_of(pz, py, pc):
        return (pz * 4 + py) * 2 + pc

    def ahead(step):
        dz, dy, dc = offset(step)
        return index_of((z + dz) % 8, (y + dy) % 4, (c + dc) % 2)

    def behind(step):
        dz, dy, dc = offset(step)
        return index_of((z + 8 - dz) % 8, (y + 4 - dy) % 4, (c + 2 - dc) % 2)

    def loop(low, high, body):
        def run(step, _):
            body(step)
            return 0
        lax.fori_loop(low, high, run, 0)

    def remote(src, dst, first, second, **device_id):
        return pltpu.make_async_remote_copy(
            src_ref=src, dst_ref=dst, send_sem=first, recv_sem=second,
            device_id=device_id, device_id_type=MESH)

    barrier = pltpu.get_barrier_semaphore()
    loop(1, n, lambda step: pl.semaphore_signal(
        barrier, inc=1, device_id={"rows": ahead(step)}, device_id_type=MESH))
    loop(1, copies, lambda step: pl.semaphore_signal(
        barrier, inc=1, device_id={"grp": (copy_id + step) % copies}, device_id_type=MESH))
    pl.semaphore_wait(barrier, n + copies - 2)

    def ask(step):
        return remote(asked.at[ahead(step)], got.at[step], ask_send.at[step], ask_recv.at[step], rows=ahead(step))

    loop(1, n, lambda step: ask(step).start())
    mine = pltpu.make_async_copy(asked.at[me], got.at[0], copy_sems.at[0])
    mine.start()

    table_copy.wait()
    share = table.shape[0] // copies
    part = 512

    def gram_part(index, acc):
        rows = table[pl.ds(pl.multiple_of(copy_id * share + index * part, part), part), :]
        return acc + lax.dot_general(rows, rows, (((0,), (0,)), ((), ())), preferred_element_type=f32)

    rank = table.shape[1]
    gram_send[:rank, :] = lax.fori_loop(0, share // part, gram_part, jnp.zeros((rank, rank), f32))
    gram_send[rank:, :] = wrong[...]
    pieces = gram_send.shape[0] // PIECE

    def piece(ref, index):
        return ref.at[pl.ds(pl.multiple_of(index * PIECE, PIECE), PIECE)]

    def gram_out(index):
        return remote(piece(gram_send, index), gram_got.at[me], gram_sems.at[0, index], gram_sems.at[1, me], rows=3 * index)

    def gram_start(index):
        @pl.when(3 * index != me)
        def _():
            gram_out(index).start()

    loop(0, pieces, gram_start)

    widen_rows(table, wide, 0)
    loop(1, n, lambda step: ask(step).wait_recv())
    mine.wait()
    first_steps = 16

    def numbers(low, count, sem):
        return pltpu.make_async_copy(got.at[pl.ds(low, count)], idx.at[pl.ds(low, count)], copy_sems.at[sem])

    numbers(0, first_steps, 0).start()
    numbers(first_steps, n - first_steps, 3).start()
    numbers(0, first_steps, 0).wait()

    def fetch(step, line, first, count, dst, at):
        for inner in range(count):
            block[pl.ds(inner, 1), :] = wide[pl.ds(idx[step, line, first + inner], 1), :]
        dst[pl.ds(at, count), :] = block[:count, :].astype(bf16)

    def serve_early(step):
        loop(0, early // LANES, lambda line: fetch(
            step, line, 0, LANES, send_early.at[step], pl.multiple_of(line * LANES, LANES)))

    def serve_late(step):
        fetch(step, early // LANES, 0, late, send_late.at[step], 0)

    def early_to(step):
        return remote(send_early.at[step], got_early.at[me], early_send.at[step], early_recv.at[step], rows=behind(step))

    def early_from(step):
        return remote(send_early.at[step], got_early.at[ahead(step)], early_send.at[step], early_recv.at[step],
                      rows=ahead(step))

    def late_to(step):
        return remote(send_late.at[step], got_late.at[me], late_send.at[step], late_recv.at[step], rows=behind(step))

    def late_from(step):
        return remote(send_late.at[step], got_late.at[ahead(step)], late_send.at[step], late_recv.at[step],
                      rows=ahead(step))

    def serve(step):
        serve_early(step)
        early_to(step).start()

    def spare_rows(step, dst):
        at, line, first = 0, cap // LANES, cap % LANES
        while at < spare:
            count = min(LANES - first, spare - at)
            fetch(step, line, first, count, dst, at)
            at, line, first = at + count, line + 1, 0

    def column(step):
        dz, dy, dc = offset(step)
        return ((y + 4 - dy) % 4) * 8 + (z + 8 - dz) % 8

    half = n // 2
    one, two, three, four, ahead_of = near
    loop(1, one, serve)
    numbers(first_steps, n - first_steps, 3).wait()
    loop(half, n, lambda step: spare_rows(step, core_send.at[column(step)]))
    core_hop = remote(core_send, core_buf.at[c], hop_sems.at[0], hop_sems.at[1], rows=index_of(z, y, 1 - c))
    core_hop.start()
    loop(one, two, serve)
    loop(0, half, lambda step: spare_rows(step, core_buf.at[c, column(step)]))
    loop(two, three, serve)
    named = hot[0, 0]
    hot_z, hot_y, hot_c = named // 8, (named // 2) % 4, named % 2

    core_hop.wait()

    def keep_core(index):
        y_send[index] = core_buf[hot_c, index]

    loop(0, half, keep_core)

    def y_hop(dy):
        py = (y + dy) % 4
        return remote(y_send.at[pl.ds(py * 8, 8)], y_buf.at[pl.ds(y * 8, 8)], hop_sems.at[2 * dy], hop_sems.at[2 * dy + 1],
                      rows=index_of(z, py, c))

    for dy in (1, 2, 3):
        y_hop(dy).start()

    loop(three, four, serve)
    for dy in (1, 2, 3):
        y_hop(dy).wait()

    def keep_y(index):
        y_buf[y * 8 + index] = y_send[y * 8 + index]

    loop(0, 8, keep_y)

    def keep_z(index):
        z_send[index] = y_buf[hot_y * 8 + index]

    loop(0, 8, keep_z)

    def z_hop(dz):
        pz = (z + dz) % 8
        return remote(z_send.at[pz], z_buf.at[z], hop_sems.at[8 + 2 * dz], hop_sems.at[9 + 2 * dz],
                      rows=index_of(pz, y, c))

    loop(1, 8, lambda dz: z_hop(dz).start())
    z_buf[z] = z_send[z]

    loop(four, n, serve)
    loop(1, n, serve_late)
    loop(1, ahead_of, lambda step: early_to(step).wait_send())

    def serve_rest(step):
        @pl.when(step + ahead_of <= n)
        def _():
            early_to(step + ahead_of - 1).wait_send()

        late_to(step).start()

    loop(1, n, serve_rest)
    serve_early(0)
    serve_late(0)
    own_early = pltpu.make_async_copy(send_early.at[0], got_early.at[me], copy_sems.at[0])
    own_late = pltpu.make_async_copy(send_late.at[0], got_late.at[me], copy_sems.at[1])
    own_early.start()
    own_late.start()

    owner = (me % 3 == 0) & (me < 3 * pieces)

    @pl.when(owner)
    def _():
        gram_got[me] = gram_send[pl.ds(pl.multiple_of(me // 3 * PIECE, PIECE), PIECE), :]

        def gram_in(index):
            @pl.when(index != me)
            def _():
                remote(piece(gram_send, 0), gram_got.at[index], gram_sems.at[0, 0], gram_sems.at[1, index],
                       rows=index).wait_recv()

        loop(0, n, gram_in)
        gram_far[copy_id] = lax.fori_loop(
            0, n, lambda index, acc: acc + gram_got[index], jnp.zeros((PIECE, rank), f32))

        def far(step):
            return remote(gram_far.at[copy_id], gram_far.at[copy_id], far_sems.at[0, step], far_sems.at[1, step],
                          grp=(copy_id + step) % copies)

        for step in range(1, 4):
            far(step).start()
        for step in range(1, 4):
            far(step).wait()
        total = gram_far[0]
        for index in range(1, 4):
            total = total + gram_far[index]
        sums[pl.ds(pl.multiple_of(me // 3 * PIECE, PIECE), PIECE), :] = total

    def spread(step):
        at = piece(sums, me // 3)
        return remote(at, at, sum_sems.at[0, step], sum_sems.at[1, me // 3], rows=ahead(step))

    @pl.when(owner)
    def _():
        loop(1, n, lambda step: spread(step).start())

    loop(1, 8, lambda dz: z_hop(dz).wait())

    def gram_sent(index):
        @pl.when(3 * index != me)
        def _():
            gram_out(index).wait_send()
            at = piece(sums, index)
            remote(at, at, sum_sems.at[0, 0], sum_sems.at[1, index], rows=3 * index).wait_recv()

    own_early.wait()
    own_late.wait()
    place_copy.wait()
    loop(1, n, lambda step: early_from(step).wait_recv())

    def widen_early(index):
        widen_rows(got_early.at[index], fetched, index * early)

    def widen_late(index):
        widen_rows(got_late.at[index], fetched, n * early + index * late)

    loop(0, n, widen_early)
    fetched[pl.ds(n * cap, spare), :] = z_buf[hot_z].astype(f32)
    users = strength.shape[0]
    build_systems(0, early_users, place, fetched, strength, rows, systems, targets)
    loop(1, n, lambda step: late_from(step).wait_recv())
    loop(0, n, widen_late)
    build_systems(early_users, users, place, fetched, strength, rows, systems, targets)
    loop(0, pieces, gram_sent)
    block[...] = gram_shared(sums, scale)
    out[...] = solve_systems(block, systems, wide, targets, vec)

    def finish(step):
        ask(step).wait_send()
        late_to(step).wait_send()

    loop(1, n, finish)

    @pl.when(owner)
    def _():
        loop(1, n, lambda step: spread(step).wait_send())


def exchange_and_solve(asked, hot, wrong, place, strength, table, early, late, early_users, copies, scale):
    owners, lines, _ = asked.shape
    rows, rank = table.shape
    users, slots = strength.shape
    cap = early + late
    spare = lines * LANES - cap
    vmem, anywhere = pl.BlockSpec(memory_space=pltpu.VMEM), pl.BlockSpec(memory_space=pl.ANY)
    dma = pltpu.SemaphoreType.DMA
    half = owners // 2
    pieces = rank // PIECE + 1
    return pl.pallas_call(
        functools.partial(exchange_kernel, early, late, spare, early_users, NEAR, scale),
        out_shape=(
            jax.ShapeDtypeStruct((users, rank), f32),
            jax.ShapeDtypeStruct((pieces * PIECE, rank), f32),
        ),
        in_specs=[vmem, pl.BlockSpec(memory_space=pltpu.SMEM), vmem, anywhere, vmem, anywhere],
        out_specs=(vmem, vmem),
        scratch_shapes=[
            pltpu.VMEM((owners, lines, LANES), i32),
            pltpu.SMEM((owners, lines, LANES), i32),
            pltpu.SMEM((users * slots,), i32),
            pltpu.VMEM((rows, rank), bf16),
            pltpu.VMEM((rows, rank), f32),
            pltpu.VMEM((LANES, rank), f32),
            pltpu.VMEM((owners, early, rank), bf16),
            pltpu.VMEM((owners, late, rank), bf16),
            pltpu.VMEM((owners, early, rank), bf16),
            pltpu.VMEM((owners, late, rank), bf16),
            pltpu.VMEM((pieces * PIECE, rank), f32),
            pltpu.VMEM((owners, PIECE, rank), f32),
            pltpu.VMEM((copies, PIECE, rank), f32),
            pltpu.VMEM((2, half, spare, rank), bf16),
            pltpu.VMEM((half, spare, rank), bf16),
            pltpu.VMEM((half, spare, rank), bf16),
            pltpu.VMEM((half, spare, rank), bf16),
            pltpu.VMEM((8, spare, rank), bf16),
            pltpu.VMEM((8, spare, rank), bf16),
            pltpu.VMEM((owners * cap + spare, rank), f32),
            pltpu.VMEM((GROUP * slots, rank), f32),
            pltpu.VMEM((users * rank, rank), f32),
            pltpu.VMEM((users, rank), f32),
            pltpu.VMEM((rank, users), f32),
            dma((owners,)), dma((owners,)), dma((owners,)), dma((owners,)), dma((owners,)), dma((owners,)),
            dma((2, owners)), dma((2, owners)), dma((2, 4)), dma((24,)), dma((4,)),
        ],
        compiler_params=pltpu.CompilerParams(collective_id=0, has_side_effects=True, vmem_limit_bytes=60 * MIB),
    )(asked, hot, wrong, place, strength, table)


def fetch_any(item_factors, rated_owner, rated_row):
    owners = lax.axis_size("rows")
    slot_owner = rated_owner.reshape(-1)
    local_row = rated_row.reshape(-1)
    slot_total = slot_owner.shape[0]
    rank = item_factors.shape[1]
    capacity = 2 * slot_total // owners
    slot_order = jnp.argsort(slot_owner, stable=True)
    sorted_owner = slot_owner[slot_order]
    owner_starts = jnp.searchsorted(sorted_owner, jnp.arange(owners, dtype=jnp.int32))
    sorted_rank = jnp.arange(slot_total, dtype=jnp.int32) - owner_starts[sorted_owner]
    sorted_place = sorted_owner * capacity + sorted_rank
    bucket_slot = jnp.zeros((slot_total,), jnp.int32).at[slot_order].set(sorted_place)
    asked_rows = jnp.zeros((owners * capacity,), jnp.int32).at[bucket_slot].set(local_row)
    asked_rows = asked_rows.reshape(owners, capacity)
    found = jnp.take(
        item_factors,
        lax.all_to_all(asked_rows, "rows", split_axis=0, concat_axis=0, tiled=True),
        axis=0,
    )
    fetched = lax.all_to_all(found, "rows", split_axis=0, concat_axis=0, tiled=True)
    return jnp.take(fetched.reshape(owners * capacity, rank), bucket_slot, axis=0)


def per_device(item_factors, rated_owner, rated_row, strength):
    user_count, slot_count = rated_owner.shape
    shard_rows, rank = item_factors.shape
    owners = lax.axis_size("rows")
    most = 2 * user_count * slot_count // owners
    early, late = most // 2, most // 8
    early_users = user_count * 3 // 4
    place, asked, hot, wrong = prepare(
        rated_owner, rated_row, owners, early, late, most - early - late, early_users)
    scale = slot_count / (shard_rows * owners)
    solved, sums = exchange_and_solve(
        asked, hot, wrong, place.reshape(-1), strength, item_factors, early, late, early_users,
        lax.axis_size("grp"), scale)

    def usual(_):
        return solved

    def any_counts(_):
        rows = fetch_any(item_factors, rated_owner, rated_row)
        return solve(jnp.arange(user_count * slot_count, dtype=jnp.int32), rows, strength, sums, scale)

    return lax.cond(sums[rank, 0] == 0.0, usual, any_counts, 0)


def solution(mesh):
    placed = (P("rows", None), P(("rows", "grp"), None), P(("rows", "grp"), None), P(("rows", "grp"), None))
    return jax.shard_map(
        per_device, mesh=mesh, in_specs=placed, out_specs=P(("rows", "grp"), None), check_vma=False
    )
```
